32 devices in a mesh: gx: 8 (over z, y), gy: 4 (over x, core).
Axes of the slice: x: 2, y: 2, z: 4, core: 2. Of those that a mesh axis runs over, the one named last changes fastest.
Arguments:
- anomalies: float32 [16384, 1024], P(('gx', 'gy')), may hold values from -50 to 50
- obs_rows: int32 [8, 256], replicated, may hold values from 0 to 6143
- obs_var: float32 [8, 256], P('gx'), may hold values from 0.5 to 20
- taper_level: int32 [8, 3, 4], replicated, may hold values from 0 to 3
Outputs:
- posterior: float32 [16384, 1024], P(('gx', 'gy'))
The draws below stay inside these ranges and needn't reach their ends.
All inputs are finite; a program needn't handle non-finite values.
Results may differ from the reference program's by a relative error of at most 0.035.
The reference program's roundings to bfloat16 on the way count: a program that leaves them out, or rounds other values in their place, can miss the bound.
Values may be sent and summed in bfloat16 or wider, within the bound.
A program may use at most 64 MiB of HBM per device.

```python
import math
import jax
import jax.numpy as jnp
from jax import lax

M = 1024
P_SIZE = 256
NCOL = 4
NS_STEPS = 12
ROWS_DEV = 512
NROWS = 16384
N_GX = 8
N_GY = 4


def draw_anomalies(key, part):
    first_key, second_key, third_key, fourth_key, fifth_key = jax.random.split(jax.random.fold_in(key, 17), 5)
    phase_shift = jax.random.uniform(fourth_key, (), jnp.float32, -math.pi, math.pi)
    angle_rows = 2.0 * math.pi / NROWS * jnp.arange(NROWS, dtype=jnp.float32)[:, None] + phase_shift
    values = jnp.clip(jax.random.normal(first_key, (NROWS, M), jnp.float32), -6.0, 6.0)
    row_scale = 0.3 * jnp.exp(jax.random.uniform(second_key, (NROWS, 1), jnp.float32, 0.0, math.log(10.0)))
    factors = jnp.clip(jax.random.normal(fifth_key, (2, M), jnp.float32), -2.5, 2.5)
    loading = 1.5
    column_scale = 0.5 * jnp.exp(jax.random.uniform(third_key, (1, M), jnp.float32, 0.0, math.log(4.0)))
    common = loading * (jnp.cos(angle_rows) * factors[0][None, :] + jnp.sin(angle_rows) * factors[1][None, :])
    return jnp.clip(row_scale * (values * column_scale + common), -49.0, 49.0).astype(jnp.float32)


def place_ends(array, own_key, least, high):
    extent = array.shape
    spot = [jax.random.randint(jax.random.fold_in(own_key, axis), (), 0, extent[axis]) for axis in range(len(extent))]
    array = array.at[tuple(spot)].set(least)
    longest = extent.index(max(extent))
    spot[longest] = (spot[longest] + 1) % extent[longest]
    return array.at[tuple(spot)].set(high)


def block_levels(own_key, shape, cuts, least, largest):
    gain = 1.0
    for axis_at, shards_of in cuts:
        draws = jax.random.uniform(jax.random.fold_in(jax.random.fold_in(own_key, 6), axis_at), (shards_of,), jnp.float32, least / len(cuts), largest / len(cuts))
        gain = gain * jnp.repeat(jnp.exp(draws), shape[axis_at] // shards_of).reshape((-1,) + (1,) * (len(shape) - 1 - axis_at))
    return gain


def setup_inputs(seed: int = 0) -> dict:
    arg_keys = jax.random.split(jax.random.key(seed), 5)
    return {
        "anomalies": draw_anomalies(jax.random.fold_in(arg_keys[4], 71), 0),
        "obs_rows": place_ends(jax.random.randint(arg_keys[1], (N_GX, P_SIZE), 0, 3 * N_GY * ROWS_DEV), jax.random.fold_in(arg_keys[1], 1), 0, (3 * N_GY * ROWS_DEV) - 1).astype(jnp.int32),
        "obs_var": jnp.clip(jnp.exp(math.log(20.0) - 3.6888795 * jax.random.uniform(arg_keys[2], (N_GX, P_SIZE), jnp.float32) ** block_levels(arg_keys[2], (N_GX, P_SIZE), ((0, 8),), -0.2, 0.2)), 0.5, 20.0),
        "taper_level": place_ends(jax.random.randint(arg_keys[3], (N_GX, 3, N_GY), 0, 4), jax.random.fold_in(arg_keys[3], 1), 0, 3).astype(jnp.int32),
    }


def mat_prod(left, right):
    return jnp.dot(left, right, precision=lax.Precision.HIGHEST, preferred_element_type=jnp.float32)

def region_rows(batch):
    columns = (batch - 1 + jnp.arange(3, dtype=jnp.int32)) % N_GX
    inside = jnp.arange(N_GY * ROWS_DEV, dtype=jnp.int32)
    return (columns[:, None] * (N_GY * ROWS_DEV) + inside[None, :]).reshape(-1).astype(jnp.int32)

def inverse_root(gram_matrix):
    identity_mat = jnp.eye(gram_matrix.shape[0], dtype=jnp.float32)
    trace_value = jnp.trace(gram_matrix)
    iter_left = gram_matrix / trace_value
    iter_right = identity_mat
    for sweep in range(NS_STEPS):
        newton_term = 1.5 * identity_mat - 0.5 * mat_prod(iter_right, iter_left)
        iter_left = mat_prod(iter_left, newton_term)
        iter_right = mat_prod(newton_term, iter_right)
    return iter_right / jnp.sqrt(trace_value)

def reference(anomalies, obs_rows, obs_var, taper_level):
    state_now = anomalies
    for colour in range(NCOL):
        batch_ids = (colour + NCOL * jnp.arange(N_GX // NCOL, dtype=jnp.int32)).astype(jnp.int32)

        def update_one(batch):
            row_ids = region_rows(batch)
            region_state = state_now[row_ids]
            observed = region_state[obs_rows[batch]].astype(jnp.bfloat16)
            gram_matrix = jnp.dot(observed, observed.T, preferred_element_type=jnp.float32) / (M - 1) + jnp.diag(obs_var[batch])
            inverse_half = inverse_root(gram_matrix).astype(jnp.bfloat16)
            transformed = jnp.dot(inverse_half, observed, preferred_element_type=jnp.float32).astype(jnp.bfloat16)
            projected = jnp.dot(region_state.astype(jnp.bfloat16), transformed.T, preferred_element_type=jnp.float32).astype(jnp.bfloat16)
            increment = jnp.dot(projected, transformed, preferred_element_type=jnp.float32)
            tapering = jnp.repeat(taper_level[batch].reshape(-1).astype(jnp.float32) / 3.0, ROWS_DEV)
            return (region_state - (tapering / (M - 1))[:, None] * increment, row_ids)
        updated, row_ids = lax.map(update_one, batch_ids)
        state_now = state_now.at[row_ids.reshape(-1)].set(updated.reshape(-1, M))
    return state_now
```

```python
import jax
import jax.numpy as jnp
from jax import lax
from jax.experimental import pallas as pl
from jax.experimental.pallas import tpu as pltpu
from jax.sharding import PartitionSpec as P

NCOL = 4
NS_STEPS = 12
SLOTS = 3
WINDOW = 8
CHUNK = 256
PIECES = 2
MESH = pl.DeviceIdType.MESH
BF16 = jnp.bfloat16
F32 = jnp.float32


class Gather:
    def __init__(self, part, var, blocks, varies, buffers, sems):
        self.part, self.var, self.blocks, self.varies = part, var, blocks, varies
        self.rec1, self.acc1, self.rec2, self.acc2, self.rec3 = buffers
        (self.s1, self.r1, self.s2, self.r2, self.s3, self.r3, self.zs, self.zr, self.ys, self.yr,
         self.xs, self.xr, self.cs, self.cr, self.vs, self.vr) = sems
        i, j = lax.axis_index("gx"), lax.axis_index("gy")
        self.i, self.j = i, j
        self.z, self.y, self.x, self.core = i // 2, i % 2, j // 2, j % 2
        self.cpart = (i, j + 1 - 2 * self.core)
        self.xpart = (i, j + 2 - 4 * self.x)
        self.ypart = (i + 1 - 2 * self.y, j)
        self.quarter = blocks.shape[4]

    def remote(self, src, dst, send, recv, who):
        return pltpu.make_async_remote_copy(
            src_ref=src, dst_ref=dst, send_sem=send, recv_sem=recv, device_id=who,
            device_id_type=MESH)

    def enter(self):
        barrier = pltpu.get_barrier_semaphore()
        greeted = [((self.i + k) % 8, self.j) for k in range(1, 8)] + [self.cpart, self.xpart]
        for who in greeted:
            pl.semaphore_signal(barrier, inc=1, device_id=who, device_id_type=MESH)
        pl.semaphore_wait(barrier, len(greeted))

    def var_copy(self, k):
        return self.remote(self.var, self.varies.at[self.i], self.vs.at[k - 1],
                           self.vr.at[self.i], ((self.i + k) % 8, self.j))

    def var_send(self):
        self.varies[self.i] = self.var[...]
        for k in range(1, 8):
            self.var_copy(k).start()

    def var_wait(self):
        for k in range(1, 8):
            n = (self.i + k) % 8
            self.remote(self.var, self.varies.at[n], self.vs.at[k - 1], self.vr.at[n],
                        self.cpart).wait_recv()

    def slot(self, colour):
        return (self.i * 3 + 1 + colour) % 4

    def copy1(self, s):
        theirs = pl.multiple_of((1 - self.core) * 2 * self.quarter, 2 * self.quarter)
        return self.remote(self.part.at[s, pl.ds(theirs, 2 * self.quarter)], self.rec1.at[s],
                           self.s1.at[s], self.r1.at[s], self.cpart)

    def copy2(self, s):
        theirs = pl.multiple_of((1 - self.x) * self.quarter, self.quarter)
        return self.remote(self.acc1.at[s, pl.ds(theirs, self.quarter)], self.rec2.at[s],
                           self.s2.at[s], self.r2.at[s], self.xpart)

    def copy3(self, s):
        n = s // 2
        return self.remote(self.acc2.at[s], self.rec3.at[n], self.s3.at[n], self.r3.at[n],
                           ((self.i + s + 7) % 8, self.j))

    def reduce0(self, colour):
        s = self.slot(colour)

        @pl.when(s < 3)
        def _():
            self.copy1(s).start()

    def reduce1(self, colour):
        s = self.slot(colour)

        @pl.when(s < 3)
        def _():
            self.copy1(s).wait_recv()
            mine = pl.multiple_of(self.core * 2 * self.quarter, 2 * self.quarter)
            self.acc1[s] = self.part[s, pl.ds(mine, 2 * self.quarter)] + self.rec1[s]
            self.copy2(s).start()

    def reduce2(self, colour):
        s = self.slot(colour)

        @pl.when(s < 3)
        def _():
            self.copy2(s).wait_recv()
            mine = pl.multiple_of(self.x * self.quarter, self.quarter)
            self.acc2[s] = self.acc1[s, pl.ds(mine, self.quarter)] + self.rec2[s]

        @pl.when(s % 2 == 0)
        def _():
            self.copy3(s).start()

    def planes(self, colour):
        f = (self.z - colour // 2 + 1) // 3
        return f, 1 - f

    def rows(self, r):
        step = self.quarter // PIECES
        return pl.ds(r * step, step)

    def block(self, colour, h, r):
        return self.blocks.at[colour // 2 + 2 * h, self.core, colour % 2, self.x, self.rows(r)]

    def copy_z(self, colour, h, r, way):
        block = self.block(colour, h, r)
        return self.remote(block, block, self.zs.at[colour, h, r, way], self.zr.at[colour, h, r],
                           ((self.i + (2, 6)[way]) % 8, self.j))

    def copy_y(self, colour, h, r):
        block = self.block(colour, h, r)
        return self.remote(block, block, self.ys.at[colour, h, r], self.yr.at[colour, h, r],
                           self.ypart)

    def copy_x(self, colour, h, r):
        block = self.block(colour, h, r)
        return self.remote(block, block, self.xs.at[colour, h, r], self.xr.at[colour, h, r],
                           self.xpart)

    def copy_core(self, colour, h, r):
        block = self.blocks.at[colour // 2 + 2 * h, self.core, colour % 2, :, self.rows(r)]
        return self.remote(block, block, self.cs.at[colour, h, r], self.cr.at[colour, h, r],
                           self.cpart)

    def spread(self, colour, h, r, wait=False):
        plane = colour // 2 + 2 * h

        @pl.when((plane <= self.z) & (self.z < 3))
        def _():
            up = self.copy_z(colour, h, r, 0)
            up.wait_send() if wait else up.start()

        @pl.when((plane >= self.z) & (self.z > 0))
        def _():
            down = self.copy_z(colour, h, r, 1)
            down.wait_send() if wait else down.start()

        side = self.copy_y(colour, h, r)
        if wait:
            side.wait_send()
        else:
            side.start()
            self.copy_x(colour, h, r).start()

    def own(self, colour):
        s = self.slot(colour)

        @pl.when(s == 1)
        def _():
            for n in range(2):
                self.remote(self.rec3.at[n], self.rec3.at[n], self.s3.at[n], self.r3.at[n],
                            self.cpart).wait_recv()
            self.blocks[self.z, self.core, self.y, self.x] = (
                self.acc2[1] + self.rec3[0] + self.rec3[1])
            for r in range(PIECES):
                self.spread(colour, self.planes(colour)[0], r)

    def near(self, colour):
        h = self.planes(colour)[0]

        @pl.when((self.y == colour % 2) & (self.slot(colour) != 1))
        def _():
            for r in range(PIECES):
                self.copy_z(colour, h, r, 0).wait_recv()
                self.spread(colour, h, r)

    def far(self, colour):
        h = self.planes(colour)[1]

        @pl.when(self.y == colour % 2)
        def _():
            for r in range(PIECES):
                self.copy_z(colour, h, r, 0).wait_recv()
                self.spread(colour, h, r)

    def side(self, colour):
        @pl.when(self.y != colour % 2)
        def _():
            for h in self.planes(colour):
                for r in range(PIECES):
                    self.copy_y(colour, h, r).wait_recv()
                    self.copy_x(colour, h, r).start()

    def cross(self, colour):
        for h in self.planes(colour):
            for r in range(PIECES):
                self.copy_x(colour, h, r).wait_recv()
                self.copy_core(colour, h, r).start()

    def arrive(self, colour):
        for h in self.planes(colour):
            for r in range(PIECES):
                self.copy_core(colour, h, r).wait_recv()

    def leave(self):
        for k in range(1, 8):
            self.var_copy(k).wait_send()
        for colour in range(NCOL):
            s = self.slot(colour)

            @pl.when(s < 3)
            def _():
                self.copy1(s).wait_send()
                self.copy2(s).wait_send()

            @pl.when(s % 2 == 0)
            def _():
                self.copy3(s).wait_send()

            @pl.when(self.y == colour % 2)
            def _():
                for h in self.planes(colour):
                    for r in range(PIECES):
                        self.spread(colour, h, r, wait=True)

            for h in self.planes(colour):
                for r in range(PIECES):
                    self.copy_x(colour, h, r).wait_send()
                    self.copy_core(colour, h, r).wait_send()


def gather_window(part, columns):
    part = lax.psum(part.astype(F32), "gy").astype(BF16)

    def shifted(block, by):
        return lax.ppermute(block, "gx", [((n + by) % columns, n) for n in range(columns)])

    whole = part[1] + shifted(part[0], 1) + shifted(part[2], -1)
    return jnp.stack([whole if n == 4 else shifted(whole, n - 4) for n in range(WINDOW)])


def split(a):
    high = a.astype(BF16)
    return high, (a - high.astype(F32)).astype(BF16)


def prod(a, b):
    ah, al = split(a)
    bh, bl = split(b)
    left = jnp.concatenate([ah, al, ah], axis=1)
    right = jnp.concatenate([bh, bh, bl], axis=0)
    return jnp.dot(left, right, preferred_element_type=F32)


def newton_step(left, right):
    lh, ll = split(left)
    rh, rl = split(right)
    p = jnp.dot(rh, lh, preferred_element_type=F32).astype(BF16)
    left_p = jnp.dot(jnp.concatenate([lh, ll], axis=1), jnp.concatenate([p, p], axis=0),
                     preferred_element_type=F32)
    p_right = jnp.dot(jnp.concatenate([p, p], axis=1), jnp.concatenate([rh, rl], axis=0),
                      preferred_element_type=F32)
    return 1.5 * left - 0.5 * left_p, 1.5 * right - 0.5 * p_right


NT = (((1,), (1,)), ((), ()))


def colours(x_ref, blocks, varies, cf_ref, out_ref, obs_ref, state, proj_ref, tr, trt, lm, rm,
            half, stages=None):
    tile_rows, members = x_ref.shape
    quarter = blocks.shape[4]
    size = 4 * quarter
    eye_mask = lax.broadcasted_iota(jnp.int32, (size, size), 0) == lax.broadcasted_iota(
        jnp.int32, (size, size), 1)
    eye = jnp.where(eye_mask, 1.0, 0.0).astype(F32)

    def newton(rl):
        return 1.5 * eye - 0.5 * rl

    def batch_rows(colour, h):
        return jnp.concatenate(
            [blocks[colour // 2 + 2 * h, core, colour % 2, x] for core in range(2)
             for x in range(2)], axis=0)

    def subtract(ref, scale, left, right):
        for n in range(0, members, CHUNK):
            inc = jnp.dot(left, right(n), preferred_element_type=F32)
            ref[:, n : n + CHUNK] = ref[:, n : n + CHUNK] - scale * inc

    def catch_up(colour, earlier):
        first = tile_rows + 2 * colour * size
        rows = state[...].astype(BF16)
        total = 0.0
        for h in range(2):
            n = 2 * earlier + h
            scale = cf_ref[first : first + 2 * size, n : n + 1]
            proj = jnp.dot(rows, trt[earlier, h], preferred_element_type=F32)
            proj_ref[:, h * size : (h + 1) * size] = jnp.where(scale > 0, proj, 0.0).astype(BF16)
            total = total + scale
        subtract(state, total, proj_ref[...], lambda n: jnp.concatenate(
            [tr[earlier, h, :, n : n + CHUNK] for h in range(2)], axis=0))

    def own_tile(colour):
        offset = (lax.axis_index("gx") + 3 * colour) % NCOL

        @pl.when(offset != 2)
        def _():
            h = half(colour, offset)
            scale = cf_ref[:tile_rows, 2 * colour : 2 * colour + 1] + cf_ref[
                :tile_rows, 2 * colour + 1 : 2 * colour + 2]
            proj = jnp.dot(out_ref[...].astype(BF16), trt[colour, h], preferred_element_type=F32)
            subtract(out_ref, scale, proj.astype(BF16), lambda n: tr[colour, h, :, n : n + CHUNK])

    stage = stages or (lambda colour, at: None)
    if stages is None:
        out_ref[...] = x_ref[...]
    for colour in range(NCOL):
        stage(colour, "start")
        for h in range(2):
            rows = batch_rows(colour, h)
            if colour:
                state[h * size : (h + 1) * size] = rows.astype(F32)
            else:
                obs_ref[h] = rows
        if colour:
            for earlier in range(colour):
                catch_up(colour, earlier)
            for h in range(2):
                obs_ref[h] = state[h * size : (h + 1) * size].astype(BF16)
        stage(colour, "caught")
        traces = []
        for h in range(2):
            obs = obs_ref[h]
            gram = lax.dot_general(obs, obs, NT, preferred_element_type=F32) / (members - 1)
            gram = gram + jnp.where(eye_mask, varies[colour + NCOL * h], 0.0)
            trace = jnp.sum(jnp.where(eye_mask, gram, 0.0))
            traces.append(trace)
            left = gram / trace
            q = newton(left)
            lm[h] = prod(left, q)
            rm[h] = q

        def step(k, carry):
            for at in range(NS_STEPS - 2):
                if stages and stages(colour, at, True):
                    @pl.when(k == at)
                    def _():
                        stages(colour, at)
            for h in range(2):
                lm[h], rm[h] = newton_step(lm[h], rm[h])
            return carry

        lax.fori_loop(0, NS_STEPS - 2, step, 0)
        stage(colour, "rooted")
        for h in range(2):
            right = rm[h]
            right = prod(newton(prod(right, lm[h])), right)
            root = (right / jnp.sqrt(traces[h])).astype(BF16)
            spread = jnp.dot(root, obs_ref[h], preferred_element_type=F32)
            tr[colour, h] = spread.astype(BF16)
            trt[colour, h] = spread.T.astype(BF16)
        stage(colour, "moved")
        own_tile(colour)


def table(*rows):
    return {row[:2]: row[2:] for row in rows}


SCHEDULE = table(
    (0, 0, ("reduce2", 2), ("far", 1)),
    (0, 4, ("side", 1), ("own", 2)),
    (0, 8, ("cross", 1), ("near", 2), ("reduce1", 3)),
    (0, "moved", ("reduce2", 3), ("far", 2)),
    (1, "start", ("arrive", 1),),
    (1, "caught", ("side", 2), ("own", 3)),
    (1, 3, ("near", 3),),
    (1, 5, ("cross", 2),),
    (1, 8, ("far", 3),),
    (2, "start", ("arrive", 2),),
    (2, "caught", ("side", 3),),
    (2, 5, ("cross", 3),),
    (3, "start", ("arrive", 3),),
)


def gathered_kernel(x_ref, part, var, cf_ref, out_ref, blocks, varies, obs_ref, state, proj_ref,
                    tr, trt, lm, rm, rec1, acc1, rec2, acc2, rec3, *sems):
    gather = Gather(part, var, blocks, varies, (rec1, acc1, rec2, acc2, rec3), sems)
    gather.enter()
    for colour in range(NCOL):
        gather.reduce0(colour)
    gather.var_send()
    gather.reduce1(0)
    gather.reduce2(0)
    out_ref[...] = x_ref[...]
    gather.own(0)
    gather.near(0)
    gather.reduce1(1)
    gather.far(0)
    gather.side(0)
    gather.reduce2(1)
    gather.own(1)
    gather.cross(0)
    gather.reduce1(2)
    gather.near(1)
    gather.var_wait()
    gather.arrive(0)

    def stages(colour, at, ask=False):
        todo = SCHEDULE.get((colour, at), ())
        if not ask:
            for name, which in todo:
                getattr(gather, name)(which)
        return bool(todo)

    def half(colour, offset):
        batch = lax.axis_index("gx") + 8 - offset + NCOL * (offset // 3)
        return batch % 8 // NCOL

    colours(x_ref, blocks, varies, cf_ref, out_ref, obs_ref, state, proj_ref, tr, trt, lm, rm,
            half, stages)
    gather.leave()


def window_kernel(*refs):
    colours(*refs, lambda colour, offset: 1 - offset % 3 % 2)


def compute_scratch(size, members):
    return [
        pltpu.VMEM((2, size, members), BF16),
        pltpu.VMEM((2 * size, members), F32),
        pltpu.VMEM((2 * size, 2 * size), BF16),
        pltpu.VMEM((NCOL, 2, size, members), BF16),
        pltpu.VMEM((NCOL, 2, members, size), BF16),
        pltpu.VMEM((2, size, size), F32),
        pltpu.VMEM((2, size, size), F32),
    ]


def gathered_call(tile, part, var, coef):
    size, members = part.shape[1:]
    quarter = size // 4
    vm = lambda *shape: pltpu.VMEM(shape, BF16)
    dma = lambda *shape: pltpu.SemaphoreType.DMA(shape)
    return pl.pallas_call(
        gathered_kernel,
        out_shape=jax.ShapeDtypeStruct(tile.shape, F32),
        in_specs=[pl.BlockSpec(memory_space=pltpu.VMEM)] * 4,
        out_specs=pl.BlockSpec(memory_space=pltpu.VMEM),
        scratch_shapes=[
            vm(4, 2, 2, 2, quarter, members), pltpu.VMEM((8, 1, size), F32),
            *compute_scratch(size, members),
            vm(3, 2 * quarter, members), vm(3, 2 * quarter, members),
            vm(3, quarter, members), vm(3, quarter, members), vm(2, quarter, members),
            dma(3), dma(3), dma(3), dma(3), dma(2), dma(2),
            dma(4, 2, PIECES, 2), *[dma(4, 2, PIECES)] * 7, dma(7), dma(8),
        ],
        compiler_params=pltpu.CompilerParams(
            collective_id=0, has_side_effects=True, vmem_limit_bytes=48 * 2**20),
    )(tile, part, var, coef)


def colours_call(tile, blocks, var, coef):
    size, members = 4 * blocks.shape[4], blocks.shape[5]
    return pl.pallas_call(
        window_kernel,
        out_shape=jax.ShapeDtypeStruct(tile.shape, F32),
        in_specs=[pl.BlockSpec(memory_space=pltpu.VMEM)] * 4,
        out_specs=pl.BlockSpec(memory_space=pltpu.VMEM),
        scratch_shapes=compute_scratch(size, members),
        compiler_params=pltpu.CompilerParams(vmem_limit_bytes=48 * 2**20),
    )(tile, blocks, var, coef)


def on_device(tile, obs_rows, obs_var, taper_level):
    tile_rows, members = tile.shape
    columns, groups = lax.axis_size("gx"), lax.axis_size("gy")
    column, group = lax.axis_index("gx"), lax.axis_index("gy")
    column_rows = groups * tile_rows
    size = obs_rows.shape[1]

    near = (column - 1 + jnp.arange(SLOTS)) % columns
    first = (2 - jnp.arange(SLOTS)) * column_rows + group * tile_rows
    local = (obs_rows[near] - first[:, None]).reshape(-1, 1)
    pick = (local == jnp.arange(tile_rows)[None, :]).astype(BF16)
    part = jnp.dot(pick, tile.astype(BF16), preferred_element_type=F32).astype(BF16)
    part = part.reshape(SLOTS, size, members)

    exact = (columns, groups) == (8, 4)
    if exact:
        batches = jnp.array([b for n in range(NCOL) for b in (n, n + NCOL)], jnp.int32)
        by_colour = lambda a: a.reshape(2, NCOL, -1).transpose(1, 0, 2).reshape(WINDOW, -1)
    else:
        window = gather_window(part, columns)
        base = (column + columns - 4) % columns
        at = (jnp.arange(NCOL) - base) % NCOL
        at = jnp.concatenate([at, at + NCOL])
        batches = (base + at) % columns
        blocks = window[at].reshape(4, 2, 2, 2, size // 4, members).transpose(0, 2, 1, 3, 4, 5)
        var = lax.all_gather(obs_var, "gx", axis=0, tiled=True)[batches][:, None]
        batches = batches.reshape(2, NCOL).T.reshape(-1)
        by_colour = lambda a: a[batches].reshape(WINDOW, -1)

    rows_w = by_colour(obs_rows)
    col_w = ((batches - 1)[:, None] + rows_w // column_rows) % columns
    tile_w = (rows_w % column_rows) // tile_rows
    col_all = jnp.concatenate([jnp.full((tile_rows,), column), col_w.reshape(-1)])
    tile_all = jnp.concatenate([jnp.full((tile_rows,), group), tile_w.reshape(-1)])
    slot = (col_all[:, None] - batches[None, :] + 1) % columns
    spot = jnp.where(slot < SLOTS, slot * groups + tile_all[:, None], -1)
    levels = by_colour(taper_level).astype(F32)
    hit = spot[:, :, None] == jnp.arange(SLOTS * groups)[None, None, :]
    coef = jnp.sum(jnp.where(hit, levels[None], 0.0), axis=-1) / 3.0 / (members - 1)
    if exact:
        return gathered_call(tile, part, obs_var, coef)
    return colours_call(tile, blocks, var, coef)


def solution(mesh):
    in_specs = (P(("gx", "gy"), None), P(), P("gx", None), P())
    out_specs = P(("gx", "gy"), None)
    return jax.shard_map(
        on_device, mesh=mesh, in_specs=in_specs, out_specs=out_specs, check_vma=False
    )
```

```python
import jax
import jax.numpy as jnp
from jax import lax
from jax.experimental import pallas as pl
from jax.experimental.pallas import tpu as pltpu
from jax.sharding import PartitionSpec as P

NCOL = 4
NS_STEPS = 12
SLOTS = 3
WINDOW = 8
CHUNK = 256
PIECES = 2
MESH = pl.DeviceIdType.MESH
BF16 = jnp.bfloat16
F32 = jnp.float32


class Gather:
    def __init__(self, part, var, blocks, varies, buffers, sems):
        self.part, self.var, self.blocks, self.varies = part, var, blocks, varies
        self.rec1, self.acc1, self.rec2, self.acc2, self.rec3 = buffers
        (self.s1, self.r1, self.s2, self.r2, self.s3, self.r3, self.zs, self.zr, self.ys, self.yr,
         self.xs, self.xr, self.cs, self.cr, self.vs, self.vr) = sems
        i, j = lax.axis_index("gx"), lax.axis_index("gy")
        self.i, self.j = i, j
        self.z, self.y, self.x, self.core = i // 2, i % 2, j // 2, j % 2
        self.cpart = (i, j + 1 - 2 * self.core)
        self.xpart = (i, j + 2 - 4 * self.x)
        self.ypart = (i + 1 - 2 * self.y, j)
        self.quarter = blocks.shape[4]

    def remote(self, src, dst, send, recv, who):
        return pltpu.make_async_remote_copy(
            src_ref=src, dst_ref=dst, send_sem=send, recv_sem=recv, device_id=who,
            device_id_type=MESH)

    def enter(self):
        barrier = pltpu.get_barrier_semaphore()
        greeted = [((self.i + k) % 8, self.j) for k in range(1, 8)] + [self.cpart, self.xpart]
        for who in greeted:
            pl.semaphore_signal(barrier, inc=1, device_id=who, device_id_type=MESH)
        pl.semaphore_wait(barrier, len(greeted))

    def var_copy(self, k):
        return self.remote(self.var, self.varies.at[self.i], self.vs.at[k - 1],
                           self.vr.at[self.i], ((self.i + k) % 8, self.j))

    def var_send(self):
        self.varies[self.i] = self.var[...]
        for k in range(1, 8):
            self.var_copy(k).start()

    def var_wait(self):
        for k in range(1, 8):
            n = (self.i + k) % 8
            self.remote(self.var, self.varies.at[n], self.vs.at[k - 1], self.vr.at[n],
                        self.cpart).wait_recv()

    def slot(self, colour):
        return (self.i * 3 + 1 + colour) % 4

    def copy1(self, s):
        theirs = pl.multiple_of((1 - self.core) * 2 * self.quarter, 2 * self.quarter)
        return self.remote(self.part.at[s, pl.ds(theirs, 2 * self.quarter)], self.rec1.at[s],
                           self.s1.at[s], self.r1.at[s], self.cpart)

    def copy2(self, s):
        theirs = pl.multiple_of((1 - self.x) * self.quarter, self.quarter)
        return self.remote(self.acc1.at[s, pl.ds(theirs, self.quarter)], self.rec2.at[s],
                           self.s2.at[s], self.r2.at[s], self.xpart)

    def copy3(self, s):
        n = s // 2
        return self.remote(self.acc2.at[s], self.rec3.at[n], self.s3.at[n], self.r3.at[n],
                           ((self.i + s + 7) % 8, self.j))

    def reduce0(self, colour):
        s = self.slot(colour)

        @pl.when(s < 3)
        def _():
            self.copy1(s).start()

    def reduce1(self, colour):
        s = self.slot(colour)

        @pl.when(s < 3)
        def _():
            self.copy1(s).wait_recv()
            mine = pl.multiple_of(self.core * 2 * self.quarter, 2 * self.quarter)
            self.acc1[s] = self.part[s, pl.ds(mine, 2 * self.quarter)] + self.rec1[s]
            self.copy2(s).start()

    def reduce2(self, colour):
        s = self.slot(colour)

        @pl.when(s < 3)
        def _():
            self.copy2(s).wait_recv()
            mine = pl.multiple_of(self.x * self.quarter, self.quarter)
            self.acc2[s] = self.acc1[s, pl.ds(mine, self.quarter)] + self.rec2[s]

        @pl.when(s % 2 == 0)
        def _():
            self.copy3(s).start()

    def planes(self, colour):
        f = (self.z - colour // 2 + 1) // 3
        return f, 1 - f

    def rows(self, r):
        step = self.quarter // PIECES
        return pl.ds(r * step, step)

    def block(self, colour, h, r):
        return self.blocks.at[colour // 2 + 2 * h, self.core, colour % 2, self.x, self.rows(r)]

    def copy_z(self, colour, h, r, way):
        block = self.block(colour, h, r)
        return self.remote(block, block, self.zs.at[colour, h, r, way], self.zr.at[colour, h, r],
                           ((self.i + (2, 6)[way]) % 8, self.j))

    def copy_y(self, colour, h, r):
        block = self.block(colour, h, r)
        return self.remote(block, block, self.ys.at[colour, h, r], self.yr.at[colour, h, r],
                           self.ypart)

    def copy_x(self, colour, h, r):
        block = self.block(colour, h, r)
        return self.remote(block, block, self.xs.at[colour, h, r], self.xr.at[colour, h, r],
                           self.xpart)

    def copy_core(self, colour, h, r):
        block = self.blocks.at[colour // 2 + 2 * h, self.core, colour % 2, :, self.rows(r)]
        return self.remote(block, block, self.cs.at[colour, h, r], self.cr.at[colour, h, r],
                           self.cpart)

    def spread(self, colour, h, r, wait=False):
        plane = colour // 2 + 2 * h

        @pl.when((plane <= self.z) & (self.z < 3))
        def _():
            up = self.copy_z(colour, h, r, 0)
            up.wait_send() if wait else up.start()

        @pl.when((plane >= self.z) & (self.z > 0))
        def _():
            down = self.copy_z(colour, h, r, 1)
            down.wait_send() if wait else down.start()

        side = self.copy_y(colour, h, r)
        if wait:
            side.wait_send()
        else:
            side.start()
            self.copy_x(colour, h, r).start()

    def own(self, colour):
        s = self.slot(colour)

        @pl.when(s == 1)
        def _():
            for n in range(2):
                self.remote(self.rec3.at[n], self.rec3.at[n], self.s3.at[n], self.r3.at[n],
                            self.cpart).wait_recv()
            self.blocks[self.z, self.core, self.y, self.x] = (
                self.acc2[1] + self.rec3[0] + self.rec3[1])
            for r in range(PIECES):
                self.spread(colour, self.planes(colour)[0], r)

    def near(self, colour):
        h = self.planes(colour)[0]

        @pl.when((self.y == colour % 2) & (self.slot(colour) != 1))
        def _():
            for r in range(PIECES):
                self.copy_z(colour, h, r, 0).wait_recv()
                self.spread(colour, h, r)

    def far(self, colour):
        h = self.planes(colour)[1]

        @pl.when(self.y == colour % 2)
        def _():
            for r in range(PIECES):
                self.copy_z(colour, h, r, 0).wait_recv()
                self.spread(colour, h, r)

    def side(self, colour):
        @pl.when(self.y != colour % 2)
        def _():
            for h in self.planes(colour):
                for r in range(PIECES):
                    self.copy_y(colour, h, r).wait_recv()
                    self.copy_x(colour, h, r).start()

    def cross(self, colour):
        for h in self.planes(colour):
            for r in range(PIECES):
                self.copy_x(colour, h, r).wait_recv()
                self.copy_core(colour, h, r).start()

    def arrive(self, colour):
        for h in self.planes(colour):
            for r in range(PIECES):
                self.copy_core(colour, h, r).wait_recv()

    def leave(self):
        for k in range(1, 8):
            self.var_copy(k).wait_send()
        for colour in range(NCOL):
            s = self.slot(colour)

            @pl.when(s < 3)
            def _():
                self.copy1(s).wait_send()
                self.copy2(s).wait_send()

            @pl.when(s % 2 == 0)
            def _():
                self.copy3(s).wait_send()

            @pl.when(self.y == colour % 2)
            def _():
                for h in self.planes(colour):
                    for r in range(PIECES):
                        self.spread(colour, h, r, wait=True)

            for h in self.planes(colour):
                for r in range(PIECES):
                    self.copy_x(colour, h, r).wait_send()
                    self.copy_core(colour, h, r).wait_send()


def gather_window(part, columns):
    part = lax.psum(part.astype(F32), "gy").astype(BF16)

    def shifted(block, by):
        return lax.ppermute(block, "gx", [((n + by) % columns, n) for n in range(columns)])

    whole = part[1] + shifted(part[0], 1) + shifted(part[2], -1)
    return jnp.stack([whole if n == 4 else shifted(whole, n - 4) for n in range(WINDOW)])


def split(a):
    high = a.astype(BF16)
    return high, (a - high.astype(F32)).astype(BF16)


def prod(a, b):
    ah, al = split(a)
    bh, bl = split(b)
    left = jnp.concatenate([ah, al, ah], axis=1)
    right = jnp.concatenate([bh, bh, bl], axis=0)
    return jnp.dot(left, right, preferred_element_type=F32)


def newton_step(left, right):
    lh, ll = split(left)
    rh, rl = split(right)
    p = jnp.dot(rh, lh, preferred_element_type=F32).astype(BF16)
    left_p = jnp.dot(jnp.concatenate([lh, ll], axis=1), jnp.concatenate([p, p], axis=0),
                     preferred_element_type=F32)
    p_right = jnp.dot(jnp.concatenate([p, p], axis=1), jnp.concatenate([rh, rl], axis=0),
                      preferred_element_type=F32)
    return 1.5 * left - 0.5 * left_p, 1.5 * right - 0.5 * p_right


NT = (((1,), (1,)), ((), ()))


def colours(x_ref, blocks, varies, cf_ref, out_ref, obs_ref, state, proj_ref, tr, trt, lm, rm,
            half, stages=None):
    tile_rows, members = x_ref.shape
    quarter = blocks.shape[4]
    size = 4 * quarter
    eye_mask = lax.broadcasted_iota(jnp.int32, (size, size), 0) == lax.broadcasted_iota(
        jnp.int32, (size, size), 1)
    eye = jnp.where(eye_mask, 1.0, 0.0).astype(F32)

    def newton(rl):
        return 1.5 * eye - 0.5 * rl

    def batch_rows(colour, h):
        return jnp.concatenate(
            [blocks[colour // 2 + 2 * h, core, colour % 2, x] for core in range(2)
             for x in range(2)], axis=0)

    def subtract(ref, scale, left, right):
        for n in range(0, members, CHUNK):
            inc = jnp.dot(left, right(n), preferred_element_type=F32)
            ref[:, n : n + CHUNK] = ref[:, n : n + CHUNK] - scale * inc

    def catch_up(colour, earlier):
        first = tile_rows + 2 * colour * size
        rows = state[...].astype(BF16)
        total = 0.0
        for h in range(2):
            n = 2 * earlier + h
            scale = cf_ref[first : first + 2 * size, n : n + 1]
            proj = jnp.dot(rows, trt[earlier, h], preferred_element_type=F32)
            proj_ref[:, h * size : (h + 1) * size] = jnp.where(scale > 0, proj, 0.0).astype(BF16)
            total = total + scale
        subtract(state, total, proj_ref[...], lambda n: jnp.concatenate(
            [tr[earlier, h, :, n : n + CHUNK] for h in range(2)], axis=0))

    def own_tile(colour):
        offset = (lax.axis_index("gx") + 3 * colour) % NCOL

        @pl.when(offset != 2)
        def _():
            h = half(colour, offset)
            scale = cf_ref[:tile_rows, 2 * colour : 2 * colour + 1] + cf_ref[
                :tile_rows, 2 * colour + 1 : 2 * colour + 2]
            proj = jnp.dot(out_ref[...].astype(BF16), trt[colour, h], preferred_element_type=F32)
            subtract(out_ref, scale, proj.astype(BF16), lambda n: tr[colour, h, :, n : n + CHUNK])

    stage = stages or (lambda colour, at: None)
    if stages is None:
        out_ref[...] = x_ref[...]
    for colour in range(NCOL):
        stage(colour, "start")
        for h in range(2):
            rows = batch_rows(colour, h)
            if colour:
                state[h * size : (h + 1) * size] = rows.astype(F32)
            else:
                obs_ref[h] = rows
        if colour:
            for earlier in range(colour):
                catch_up(colour, earlier)
            for h in range(2):
                obs_ref[h] = state[h * size : (h + 1) * size].astype(BF16)
        stage(colour, "caught")
        traces = []
        for h in range(2):
            obs = obs_ref[h]
            gram = lax.dot_general(obs, obs, NT, preferred_element_type=F32) / (members - 1)
            gram = gram + jnp.where(eye_mask, varies[colour + NCOL * h], 0.0)
            trace = jnp.sum(jnp.where(eye_mask, gram, 0.0))
            traces.append(trace)
            left = gram / trace
            q = newton(left)
            lm[h] = prod(left, q)
            rm[h] = q

        def step(k, carry):
            for at in range(NS_STEPS - 2):
                if stages and stages(colour, at, True):
                    @pl.when(k == at)
                    def _():
                        stages(colour, at)
            for h in range(2):
                lm[h], rm[h] = newton_step(lm[h], rm[h])
            return carry

        lax.fori_loop(0, NS_STEPS - 2, step, 0)
        stage(colour, "rooted")
        for h in range(2):
            right = rm[h]
            right = prod(newton(prod(right, lm[h])), right)
            root = (right / jnp.sqrt(traces[h])).astype(BF16)
            spread = jnp.dot(root, obs_ref[h], preferred_element_type=F32)
            tr[colour, h] = spread.astype(BF16)
            trt[colour, h] = spread.T.astype(BF16)
        stage(colour, "moved")
        own_tile(colour)


def table(*rows):
    return {row[:2]: row[2:] for row in rows}


SCHEDULE = table(
    (0, "caught", ("own", 2)),
    (0, 2, ("side", 1), ("reduce2", 3)),
    (0, 5, ("near", 2)),
    (0, 7, ("cross", 1)),
    (0, "rooted", ("own", 3)),
    (0, "moved", ("far", 2)),
    (1, "start", ("arrive", 1)),
    (1, "caught", ("near", 3), ("side", 2)),
    (1, 4, ("far", 3)),
    (1, 6, ("cross", 2)),
    (2, "start", ("arrive", 2)),
    (2, "caught", ("side", 3)),
    (2, 5, ("cross", 3)),
    (3, "start", ("arrive", 3)),
)


def gathered_kernel(x_ref, part, var, cf_ref, out_ref, blocks, varies, obs_ref, state, proj_ref,
                    tr, trt, lm, rm, rec1, acc1, rec2, acc2, rec3, *sems):
    gather = Gather(part, var, blocks, varies, (rec1, acc1, rec2, acc2, rec3), sems)
    gather.enter()
    for colour in range(NCOL):
        gather.reduce0(colour)
    gather.var_send()
    gather.reduce1(0)
    gather.reduce2(0)
    out_ref[...] = x_ref[...]
    gather.own(0)
    gather.reduce1(1)
    gather.near(0)
    gather.reduce2(1)
    gather.far(0)
    gather.own(1)
    gather.side(0)
    gather.reduce1(2)
    gather.near(1)
    gather.cross(0)
    gather.reduce2(2)
    gather.far(1)
    gather.reduce1(3)
    gather.var_wait()
    gather.arrive(0)

    def stages(colour, at, ask=False):
        todo = SCHEDULE.get((colour, at), ())
        if not ask:
            for name, which in todo:
                getattr(gather, name)(which)
        return bool(todo)

    def half(colour, offset):
        batch = lax.axis_index("gx") + 8 - offset + NCOL * (offset // 3)
        return batch % 8 // NCOL

    colours(x_ref, blocks, varies, cf_ref, out_ref, obs_ref, state, proj_ref, tr, trt, lm, rm,
            half, stages)
    gather.leave()


def window_kernel(*refs):
    colours(*refs, lambda colour, offset: 1 - offset % 3 % 2)


def compute_scratch(size, members):
    return [
        pltpu.VMEM((2, size, members), BF16),
        pltpu.VMEM((2 * size, members), F32),
        pltpu.VMEM((2 * size, 2 * size), BF16),
        pltpu.VMEM((NCOL, 2, size, members), BF16),
        pltpu.VMEM((NCOL, 2, members, size), BF16),
        pltpu.VMEM((2, size, size), F32),
        pltpu.VMEM((2, size, size), F32),
    ]


def gathered_call(tile, part, var, coef):
    size, members = part.shape[1:]
    quarter = size // 4
    vm = lambda *shape: pltpu.VMEM(shape, BF16)
    dma = lambda *shape: pltpu.SemaphoreType.DMA(shape)
    return pl.pallas_call(
        gathered_kernel,
        out_shape=jax.ShapeDtypeStruct(tile.shape, F32),
        in_specs=[pl.BlockSpec(memory_space=pltpu.VMEM)] * 4,
        out_specs=pl.BlockSpec(memory_space=pltpu.VMEM),
        scratch_shapes=[
            vm(4, 2, 2, 2, quarter, members), pltpu.VMEM((8, 1, size), F32),
            *compute_scratch(size, members),
            vm(3, 2 * quarter, members), vm(3, 2 * quarter, members),
            vm(3, quarter, members), vm(3, quarter, members), vm(2, quarter, members),
            dma(3), dma(3), dma(3), dma(3), dma(2), dma(2),
            dma(4, 2, PIECES, 2), *[dma(4, 2, PIECES)] * 7, dma(7), dma(8),
        ],
        compiler_params=pltpu.CompilerParams(
            collective_id=0, has_side_effects=True, vmem_limit_bytes=48 * 2**20),
    )(tile, part, var, coef)


def colours_call(tile, blocks, var, coef):
    size, members = 4 * blocks.shape[4], blocks.shape[5]
    return pl.pallas_call(
        window_kernel,
        out_shape=jax.ShapeDtypeStruct(tile.shape, F32),
        in_specs=[pl.BlockSpec(memory_space=pltpu.VMEM)] * 4,
        out_specs=pl.BlockSpec(memory_space=pltpu.VMEM),
        scratch_shapes=compute_scratch(size, members),
        compiler_params=pltpu.CompilerParams(vmem_limit_bytes=48 * 2**20),
    )(tile, blocks, var, coef)


def on_device(tile, obs_rows, obs_var, taper_level):
    tile_rows, members = tile.shape
    columns, groups = lax.axis_size("gx"), lax.axis_size("gy")
    column, group = lax.axis_index("gx"), lax.axis_index("gy")
    column_rows = groups * tile_rows
    size = obs_rows.shape[1]

    near = (column - 1 + jnp.arange(SLOTS)) % columns
    first = (2 - jnp.arange(SLOTS)) * column_rows + group * tile_rows
    local = (obs_rows[near] - first[:, None]).reshape(-1, 1)
    pick = (local == jnp.arange(tile_rows)[None, :]).astype(BF16)
    part = jnp.dot(pick, tile.astype(BF16), preferred_element_type=F32).astype(BF16)
    part = part.reshape(SLOTS, size, members)

    exact = (columns, groups) == (8, 4)
    if exact:
        batches = jnp.array([b for n in range(NCOL) for b in (n, n + NCOL)], jnp.int32)
        by_colour = lambda a: a.reshape(2, NCOL, -1).transpose(1, 0, 2).reshape(WINDOW, -1)
    else:
        window = gather_window(part, columns)
        base = (column + columns - 4) % columns
        at = (jnp.arange(NCOL) - base) % NCOL
        at = jnp.concatenate([at, at + NCOL])
        batches = (base + at) % columns
        blocks = window[at].reshape(4, 2, 2, 2, size // 4, members).transpose(0, 2, 1, 3, 4, 5)
        var = lax.all_gather(obs_var, "gx", axis=0, tiled=True)[batches][:, None]
        batches = batches.reshape(2, NCOL).T.reshape(-1)
        by_colour = lambda a: a[batches].reshape(WINDOW, -1)

    rows_w = by_colour(obs_rows)
    col_w = ((batches - 1)[:, None] + rows_w // column_rows) % columns
    tile_w = (rows_w % column_rows) // tile_rows
    col_all = jnp.concatenate([jnp.full((tile_rows,), column), col_w.reshape(-1)])
    tile_all = jnp.concatenate([jnp.full((tile_rows,), group), tile_w.reshape(-1)])
    slot = (col_all[:, None] - batches[None, :] + 1) % columns
    spot = jnp.where(slot < SLOTS, slot * groups + tile_all[:, None], -1)
    levels = by_colour(taper_level).astype(F32)
    hit = spot[:, :, None] == jnp.arange(SLOTS * groups)[None, None, :]
    coef = jnp.sum(jnp.where(hit, levels[None], 0.0), axis=-1) / 3.0 / (members - 1)
    if exact:
        return gathered_call(tile, part, obs_var, coef)
    return colours_call(tile, blocks, var, coef)


def solution(mesh):
    in_specs = (P(("gx", "gy"), None), P(), P("gx", None), P())
    out_specs = P(("gx", "gy"), None)
    return jax.shard_map(
        on_device, mesh=mesh, in_specs=in_specs, out_specs=out_specs, check_vma=False
    )
```
